256 devices in a mesh: blk: 16 (over x_lo, z), rep: 16 (over y, x_hi, core).
Axes of the slice: x: 4 (x_hi: 2, x_lo: 2; x = x_hi * 2 + x_lo), y: 4, z: 8, core: 2. Of those that a mesh axis runs over, the one named last changes fastest.
Arguments:
- a_blocks: bfloat16 [48, 16, 6, 128, 128], P('blk', None, None, None, 'rep'), may hold values from -0.5 to 0.5
- a_cols: int32 [48, 16, 6], P('blk'), may hold values from 0 to 111, as said below
- b_blocks: bfloat16 [1792, 16, 3, 128, 128], P('blk', 'rep'), may hold values from -6 to 6
- b_cols: int32 [1792, 16, 3], P('blk', 'rep'), may hold values from 0 to 111, as said below
- c_cols: int32 [48, 16, 4], P(None, 'rep'), may hold values from 0 to 111, as said below
Outputs:
- c_blocks: float32 [48, 16, 4, 128, 128], P('blk', 'rep')
The draws below stay inside these ranges and needn't reach their ends.
Inputs may be any that keep to these rules, and one draw needn't show every extreme that they name: `a_cols`: within each block row and panel the 6 entries are distinct. `b_cols`: within each block row and tile the 3 entries are distinct. `c_cols`: within each block row and tile the 4 entries are distinct.
All inputs are finite; a program needn't handle non-finite values.
Results may differ from the reference program's by a relative error of at most 0.0003.
Values may be sent and summed in bfloat16 or wider, within the bound.
A program may use at most 128 MiB of HBM per device.

```python
import jax
import jax.numpy as jnp
from jax import lax

BS = 128
KP = 112
KA = 6
KB = 3
KC = 4
PANELS = 16
TILES = 16
NROW = 48
NB = 1792
CT = 112


def distinct_lists(key, rows, middle, pool, count):
    scores = jax.random.randint(key, (rows, middle, pool), 0, 65536) * pool + jnp.arange(pool, dtype=jnp.int32)
    order = jnp.argsort(scores, axis=-1)[:, :, :count].astype(jnp.int32)
    order = order.at[0, 0].set(pool - 1 - jnp.arange(count, dtype=jnp.int32))
    order = order.at[1, 0].set(jnp.arange(count, dtype=jnp.int32))
    return order


def draw_a_cols(key, part):
    return distinct_lists(jax.random.fold_in(key, 11), NROW, PANELS, KP, KA)


def pick_window(key, salt, rows, count):
    span = 2 * max(KB, KC)
    base = jax.random.fold_in(key, 0)
    offsets = jax.random.randint(jax.random.fold_in(base, 99), (TILES,), 0, CT - span + 1).astype(jnp.int32)
    scores = jax.random.randint(jax.random.fold_in(base, salt), (rows, TILES, span), 0, 65536) * span + jnp.arange(span, dtype=jnp.int32)
    order = jnp.argsort(scores, axis=-1)[:, :, :count].astype(jnp.int32) + offsets[None, :, None]
    order = order.at[0, 0].set(CT - 1 - jnp.arange(count, dtype=jnp.int32))
    order = order.at[1, 0].set(jnp.arange(count, dtype=jnp.int32))
    return order.astype(jnp.int32)


def draw_b_cols(key, part):
    return pick_window(key, 23, NB, KB)


def draw_c_cols(key, part):
    return pick_window(key, 37, NROW, KC)


def block_scale(stream_key, shape, cuts, low, top_value):
    gain, own = 1.0, jax.random.fold_in(stream_key, 6)
    for dim, blocks in cuts:
        draws = jnp.exp(jax.random.uniform(jax.random.fold_in(own, dim), (blocks,), jnp.float32, low / len(cuts), top_value / len(cuts)))
        gain = gain * jnp.repeat(draws, shape[dim] // blocks).reshape([-1 if axis == dim else 1 for axis in range(len(shape))])
    return gain


def scatter_about(stream_key, extent, scale, reach, shards=(), kind=jnp.bfloat16):
    result = scale * jax.random.normal(stream_key, extent, jnp.float32)
    if shards:
        result = result * block_scale(stream_key, extent, shards, -0.22, 0.18)
    return jnp.clip(result, -reach, reach).astype(kind)


def setup_inputs(seed: int = 0) -> dict:
    splits = jax.random.split(jax.random.key(seed), 6)
    a_blocks = scatter_about(splits[0], (NROW, PANELS, KA, BS, BS), BS ** -0.5, 0.5, ((0, 16), (4, 16)))
    a_cols = draw_a_cols(jax.random.fold_in(splits[5], 71), 0)
    b_blocks = scatter_about(splits[2], (NB, TILES, KB, BS, BS), 1.0, 6.0, ((0, 16), (1, 16)))
    b_cols = draw_b_cols(jax.random.fold_in(splits[5], 71), 0)
    c_cols = draw_c_cols(jax.random.fold_in(splits[5], 71), 0)
    return dict(a_blocks=a_blocks, a_cols=a_cols, b_blocks=b_blocks, b_cols=b_cols, c_cols=c_cols)


def reference(a_blocks, a_cols, b_blocks, b_cols, c_cols):
    panel_base = (jnp.arange(PANELS, dtype=jnp.int32) * KP)[:, None]
    slots = PANELS * KA

    def one_row(items):
        a_row, cols_row, pattern_row = items
        global_k = (cols_row.astype(jnp.int32) + panel_base).reshape(slots).astype(jnp.int32)
        chosen = b_blocks[global_k]
        chosen_cols = b_cols[global_k]
        hits = chosen_cols[:, :, :, None] == pattern_row[None, :, None, :]
        picked = jnp.zeros((slots, TILES, KC, BS, BS), b_blocks.dtype)
        for slot_t in range(KB):
            picked = picked + jnp.where(hits[:, :, slot_t, :, None, None], chosen[:, :, slot_t, None], jnp.zeros((), b_blocks.dtype))
        left = a_row.reshape(slots, BS, BS).astype(jnp.float32)
        return jnp.einsum("sab,srcbd->rcad", left, picked.astype(jnp.float32))

    return lax.map(one_row, (a_blocks, a_cols, c_cols))
```

```python
import jax
import jax.numpy as jnp
from jax import lax
from jax.experimental import pallas as pl
from jax.experimental.pallas import tpu as pltpu
from jax.sharding import PartitionSpec as P

MESH = pl.DeviceIdType.MESH
NX, NZ = 2, 8
NY, NXH, NC = 4, 2, 2
NREP = NY * NXH * NC
ROWS, KA, KB, KC, BS, KP = 3, 6, 3, 4, 128, 112
HALF = BS // 2
PIECE = KA * BS // NREP
BLOCKS = ROWS * 2
ZERO = KP * KB
Z_SENDS, X_SENDS = 21, 9
Z_RECVS, X_RECVS = 24, 9
DUMMY = Z_RECVS + X_RECVS
FAR, NEAR, DONE = 0, 1, 2
FIRST_COL = (0, 0, 2)


def step_of(e):
    far = (8 - e) // 2
    return far * (2 * (e % 2) - 1) + NZ


def kernel(
    a_ref, cols_ref, b_hbm, table_hbm, out_ref,
    g, b, picked, part, cols_v, cols_s, table_s, sd, ss, rd, rs,
    ga_send, ga_recv, gc_send, gc_recv, cols_sem, load_sem,
    rep_send, rep_recv, d_send, s_send, d_recv, s_recv,
):
    q, t = lax.axis_index("blk"), lax.axis_index("rep")
    xl, z = q // NZ, q % NZ
    y, xh, core = t // (NXH * NC), (t // NC) % NXH, t % NC

    def blk_at(x, zz):
        return (x * NZ + zz % NZ, t)

    def slot(yy, h, c):
        return (yy % NY) * (NXH * NC) + h * NC + c

    def rep_at(yy, h, c):
        return (q, slot(yy, h, c))

    load_b = pltpu.make_async_copy(b_hbm, b.at[pl.ds(0, ZERO)], load_sem.at[0])
    load_t = pltpu.make_async_copy(table_hbm, table_s, load_sem.at[1])
    load_b.start()
    load_t.start()
    own_a = pltpu.make_async_copy(a_ref.at[:, q], g.at[t, 7, 0], load_sem.at[2])
    own_c = pltpu.make_async_copy(cols_ref.at[q], cols_v.at[7, 0], load_sem.at[3])
    own_a.start()
    own_c.start()

    barrier = pltpu.get_barrier_semaphore()

    def greet(n, carry):
        pl.semaphore_signal(barrier, inc=1, device_id=((q + n) % (NX * NZ), t), device_id_type=MESH)
        return carry

    lax.fori_loop(1, NX * NZ, greet, 0)
    for peer in (rep_at(y, 1 - xh, core), rep_at(y, xh, 1 - core), rep_at(y + 1, xh, core), rep_at(y + 2, xh, core), rep_at(y + 3, xh, core)):
        pl.semaphore_signal(barrier, inc=1, device_id=peer, device_id_type=MESH)
    pl.semaphore_wait(barrier, NX * NZ - 1 + 5)

    def over_blk(n):
        e, rel = n // 2, n % 2 + n // 14
        x, zz = (xl + rel) % NX, (z + 2 * NZ - step_of(e)) % NZ
        to = x * NZ + zz
        return (
            pltpu.make_async_remote_copy(
                a_ref.at[:, to], g.at[t, e, rel], ga_send.at[e, rel], ga_recv.at[e, rel], device_id=(to, t), device_id_type=MESH
            ),
            pltpu.make_async_remote_copy(
                cols_ref.at[to], cols_v.at[e, rel], gc_send.at[e, rel], gc_recv.at[e, rel], device_id=(to, t), device_id_type=MESH
            ),
        )

    def send_blk(n, carry):
        for copy in over_blk(n):
            copy.start()
        return carry

    lax.fori_loop(0, 15, send_blk, 0)

    b[ZERO] = jnp.zeros((BS, BS), b.dtype)
    rd[DUMMY] = jnp.zeros(rd.shape[1:], rd.dtype)
    rs[DUMMY] = jnp.zeros(rs.shape[1:], rs.dtype)

    def over_rep(e, piece, n, to):
        return pltpu.make_async_remote_copy(
            g.at[piece, e], g.at[piece, e], rep_send.at[e, n], rep_recv.at[e, piece], device_id=to, device_id_type=MESH
        )

    def arrived(e, piece):
        over_rep(e, piece, 0, rep_at(y, xh, 1 - core)).wait_recv()

    def first_sends(e):
        own = slot(y, xh, core)
        yield over_rep(e, own, 0, rep_at(y, 1 - xh, core))
        yield over_rep(e, own, 1, rep_at(y + 1, xh, core))
        yield over_rep(e, own, 2, rep_at(y + 3, xh, core))
        yield over_rep(e, own, 3, rep_at(y + 2, xh, core))
        yield over_rep(e, own, 4, rep_at(y, xh, 1 - core))

    def second_sends(e):
        other = slot(y, 1 - xh, core)
        yield over_rep(e, other, 5, rep_at(y + 1, xh, core))
        yield over_rep(e, other, 6, rep_at(y + 3, xh, core))
        yield over_rep(e, other, 7, rep_at(y + 2, xh, core))
        yield over_rep(e, other, 8, rep_at(y, xh, 1 - core))

    def third_sends(e):
        n = 9
        for d in (1, 3, 2):
            for h in (0, 1):
                piece = slot(y + d, (xh + h) % NXH, core)
                arrived(e, piece)
                yield over_rep(e, piece, n, rep_at(y, xh, 1 - core))
                n += 1

    def stage_a(e):
        for rel in (1, 0):
            def remote():
                copies = over_blk(2 * e + rel - e // 7)
                for copy in copies:
                    copy.wait_recv()

            if rel:
                remote()
            else:
                pl.when(e < 7)(remote)

                @pl.when(e == 7)
                def _():
                    own_a.wait()
                    own_c.wait()

        pltpu.make_async_copy(cols_v.at[e], cols_s.at[e], cols_sem.at[e]).start()
        for copy in first_sends(e):
            copy.start()

    def stage_b(e):
        arrived(e, slot(y, 1 - xh, core))
        for copy in second_sends(e):
            copy.start()

    def stage_c(e):
        for copy in third_sends(e):
            copy.start()

    def multiply(e):
        for yy in range(NY):
            for h in range(NXH):
                arrived(e, slot(yy, h, 1 - core))
        pltpu.make_async_copy(cols_v.at[e], cols_s.at[e], cols_sem.at[e]).wait()

        def one_row(n, carry):
            rel, r = n // ROWS, n % ROWS
            owner = ((xl + rel) % NX) * NZ + (z + step_of(e)) % NZ
            row = (owner * ROWS + r) * KC
            for s in range(KA):
                k = cols_s[e, rel, 0, r * KA + s]
                for c in range(KC):
                    which = table_s[row + c, k]
                    picked[pl.ds(s * BS, BS), pl.ds(c * BS, BS)] = b[which]
            left = g[:, e, rel, r].astype(jnp.float32).reshape(NREP, KA, BS // NREP, BS)
            left = jnp.concatenate([left[:, s].reshape(BS, BS) for s in range(KA)], axis=0).astype(b.dtype)
            total = lax.dot_general(left, picked[...], (((0,), (0,)), ((), ())), preferred_element_type=jnp.float32)
            for c in range(KC):
                part[rel, r, c] = total[:, c * BS : (c + 1) * BS]
            return carry

        lax.fori_loop(0, 2 * ROWS, one_row, 0)

    def message(frm, to_slot, to):
        return (
            pltpu.make_async_remote_copy(sd.at[frm], rd.at[to_slot], d_send.at[frm], d_recv.at[to_slot], device_id=to, device_id_type=MESH),
            pltpu.make_async_remote_copy(ss.at[frm], rs.at[to_slot], s_send.at[frm], s_recv.at[to_slot], device_id=to, device_id_type=MESH),
        )

    def received(at):
        for copy in message(0, at, blk_at(1 - xl, z)):
            copy.wait_recv()

    def totals(rel, first_col, at, j):
        r, c = j // 2, first_col + j % 2
        low, high = part[rel, r, c, pl.ds(0, HALF)], part[rel, r, c, pl.ds(HALF, HALF)]
        for n in at:
            word, scale = rd[n, j], rs[n, pl.ds(j, 1)]
            low += ((word & 0xFFFF).astype(jnp.float32) - 32768.0) * scale
            high += (lax.shift_right_logical(word, 16).astype(jnp.float32) - 32768.0) * scale
        return low, high

    def pack(rel, first_col, at, to_slot):
        def one(j, carry):
            low, high = totals(rel, first_col, at, j)
            top = jnp.maximum(jnp.max(jnp.maximum(jnp.abs(low), jnp.abs(high)), axis=0, keepdims=True), 1e-33)
            gain = 32767.0 / top
            low = (low * gain + 32768.5).astype(jnp.int32)
            high = (high * gain + 32768.5).astype(jnp.int32)
            sd[to_slot, j] = low | (high << 16)
            ss[to_slot, pl.ds(j, 1)] = top * (1.0 / 32767.0)
            return carry

        lax.fori_loop(0, BLOCKS, one, 0)

    def keep(first_col, at):
        def one(j, carry):
            low, high = totals(0, first_col, at, j)
            r, c = j // 2, first_col + j % 2
            out_ref[r, c, pl.ds(0, HALF)] = low
            out_ref[r, c, pl.ds(HALF, HALF)] = high
            return carry

        lax.fori_loop(0, BLOCKS, one, 0)

    def z_slot(e, kind):
        return (e - 1) * 3 + kind

    def along_z(e, kind):
        up = jnp.where(e == 0, jnp.int32(kind != NEAR), e % 2)
        at = jnp.where(e == 0, 2 - up, e + 2)
        return message(e * 3 + kind, z_slot(at, kind), blk_at(xl, z + NZ + 2 * up - 1))

    def has_z(e, kind):
        return (e >= 3) | (e == (2 if kind == NEAR else 1))

    def pass_on(e, kind):
        at = [jnp.where(has_z(e, kind), z_slot(e, kind), DUMMY)]
        if kind == DONE:
            received(Z_RECVS + e)
            at.append(Z_RECVS + e)

        @pl.when(has_z(e, kind))
        def _():
            received(z_slot(e, kind))

        pack(int(kind == FAR), FIRST_COL[kind], at, e * 3 + kind)
        for copy in along_z(e, kind):
            copy.start()

    def across_x(n):
        return message(Z_SENDS + n, Z_RECVS + n, blk_at(1 - xl, z))

    def send_x(n, at, first_col):
        pack(1, first_col, at, Z_SENDS + n)
        for copy in across_x(n):
            copy.start()

    load_b.wait()
    load_t.wait()

    def one_step(i, carry):
        pl.when(i < 8)(lambda: stage_a(i))
        pl.when((i >= 1) & (i < 9))(lambda: stage_b(i - 1))

        @pl.when(i >= 2)
        def _():
            e = i - 2
            stage_c(e)
            pl.when(e >= 1)(lambda: pass_on(e - 1, DONE))
            multiply(e)
            send_x(e, [], FIRST_COL[DONE])

            @pl.when(e < 7)
            def _():
                pass_on(e, FAR)
                pass_on(e, NEAR)

        return carry

    lax.fori_loop(0, 10, one_step, 0)

    for kind in (FAR, DONE, NEAR):
        for e in (7, 8):
            received(z_slot(e, kind))
        at = [z_slot(7, kind), z_slot(8, kind)]
        if kind == FAR:
            send_x(8, at, FIRST_COL[kind])
        else:
            last = Z_RECVS + (7 if kind == DONE else 8)
            received(last)
            keep(FIRST_COL[kind], at + [last])

    def sent_blk(n, carry):
        for copy in over_blk(n):
            copy.wait_send()
        return carry

    lax.fori_loop(0, 15, sent_blk, 0)

    def sent_rep(e, carry):
        for n in range(9 + 6):
            over_rep(e, t, n, rep_at(y, xh, 1 - core)).wait_send()
        return carry

    lax.fori_loop(0, 8, sent_rep, 0)

    def sent_messages(n, carry):
        for copy in message(n, 0, blk_at(1 - xl, z)):
            copy.wait_send()
        return carry

    lax.fori_loop(0, Z_SENDS + X_SENDS, sent_messages, 0)


def per_device(a_blocks, a_cols, b_blocks, b_cols, c_cols):
    panels = a_blocks.shape[1]
    pieces = jnp.swapaxes(a_blocks, 3, 4).reshape(ROWS, panels, PIECE, BS)
    lists = jnp.swapaxes(a_cols, 0, 1).reshape(panels, 1, ROWS * KA)
    lists = jnp.pad(lists, ((0, 0), (0, 7), (0, 128 - ROWS * KA)))
    wanted = c_cols[:, 0].reshape(-1, 1)
    have = b_cols[:, 0]
    table = jnp.full((wanted.shape[0], KP), ZERO, jnp.int32)
    for slot_t in range(KB):
        table = jnp.where(have[:, slot_t][None, :] == wanted, jnp.arange(KP, dtype=jnp.int32) * KB + slot_t, table)
    table = jnp.pad(table, ((0, 0), (0, 128 - KP)))
    any_ref = pl.BlockSpec(memory_space=pl.ANY)
    vmem = pltpu.VMEM
    dma = pltpu.SemaphoreType.DMA
    mine = pl.pallas_call(
        kernel,
        out_shape=jax.ShapeDtypeStruct((ROWS, KC, BS, BS), jnp.float32),
        in_specs=[any_ref] * 4,
        out_specs=pl.BlockSpec(memory_space=pltpu.VMEM),
        scratch_shapes=[
            vmem((NREP, 8, 2, ROWS, PIECE, BS), jnp.bfloat16),
            vmem((ZERO + 1, BS, BS), jnp.bfloat16),
            vmem((KA * BS, KC * BS), jnp.bfloat16),
            vmem((2, ROWS, KC, BS, BS), jnp.float32),
            vmem((8, 2, 8, 128), jnp.int32),
            pltpu.SMEM((8, 2, 8, 128), jnp.int32),
            pltpu.SMEM((table.shape[0], 128), jnp.int32),
            vmem((Z_SENDS + X_SENDS, BLOCKS, HALF, BS), jnp.int32),
            vmem((Z_SENDS + X_SENDS, 8, BS), jnp.float32),
            vmem((DUMMY + 1, BLOCKS, HALF, BS), jnp.int32),
            vmem((DUMMY + 1, 8, BS), jnp.float32),
            dma((8, 2)), dma((8, 2)), dma((8, 2)), dma((8, 2)), dma((8,)), dma((4,)),
            dma((8, 15)), dma((8, NREP)),
            dma((Z_SENDS + X_SENDS,)), dma((Z_SENDS + X_SENDS,)), dma((DUMMY,)), dma((DUMMY,)),
        ],
        compiler_params=pltpu.CompilerParams(collective_id=0, has_side_effects=True, vmem_limit_bytes=56 * 2**20),
        name="block_product",
    )(pieces, lists, b_blocks.reshape(KP * KB, BS, BS), table)
    return mine.reshape(ROWS, 1, KC, BS, BS)


def solution(mesh):
    placed = (
        P("blk", None, None, None, "rep"),
        P("blk", None, None),
        P("blk", "rep", None, None, None),
        P("blk", "rep", None),
        P(None, "rep", None),
    )
    return jax.shard_map(
        per_device,
        mesh=mesh,
        in_specs=placed,
        out_specs=P("blk", "rep", None, None, None),
        check_vma=False,
    )
```

```python
import jax
import jax.numpy as jnp
from jax import lax
from jax.experimental import pallas as pl
from jax.experimental.pallas import tpu as pltpu
from jax.sharding import PartitionSpec as P

MESH = pl.DeviceIdType.MESH
NX, NZ = 2, 8
NY, NXH, NC = 4, 2, 2
NREP = NY * NXH * NC
ROWS, KA, KB, KC, BS, KP = 3, 6, 3, 4, 128, 112
HALF = BS // 2
PIECE = KA * BS // NREP
BLOCKS = ROWS * 2
ZERO = KP * KB
Z_SENDS, X_SENDS = 21, 9
Z_RECVS, X_RECVS = 24, 9
DUMMY = Z_RECVS + X_RECVS
FAR, NEAR, DONE = 0, 1, 2
FIRST_COL = (0, 0, 2)
LEAD_A, LEAD_B, LEAD_C, LEAD_D = 4, 3, 2, 1
AHEAD = 4


def step_of(e):
    far = (8 - e) // 2
    return far * (2 * (e % 2) - 1) + NZ


def kernel(
    a_ref, cols_ref, b_hbm, table_hbm, out_ref,
    g, b, picked, part, cols_v, cols_s, table_s, sd, ss, rd, rs,
    ga_send, ga_recv, gc_send, gc_recv, cols_sem, load_sem,
    rep_send, rep_recv, d_send, s_send, d_recv, s_recv,
):
    q, t = lax.axis_index("blk"), lax.axis_index("rep")
    xl, z = q // NZ, q % NZ
    y, xh, core = t // (NXH * NC), (t // NC) % NXH, t % NC

    def blk_at(x, zz):
        return (x * NZ + zz % NZ, t)

    def rep_at(yy, h, c):
        return (q, (yy % NY) * (NXH * NC) + h * NC + c)

    def slot(yy, h, c):
        return c * (NY * NXH) + (yy % NY) * NXH + h

    me = slot(y, xh, core)

    load_b = pltpu.make_async_copy(b_hbm, b.at[pl.ds(0, ZERO)], load_sem.at[0])
    load_t = pltpu.make_async_copy(table_hbm, table_s, load_sem.at[1])
    load_b.start()
    load_t.start()
    own_a = pltpu.make_async_copy(a_ref.at[:, q], g.at[me, 7, 0], load_sem.at[2])
    own_c = pltpu.make_async_copy(cols_ref.at[q], cols_v.at[7, 0], load_sem.at[3])
    own_a.start()
    own_c.start()

    barrier = pltpu.get_barrier_semaphore()

    def greet(n, carry):
        pl.semaphore_signal(barrier, inc=1, device_id=((q + n) % (NX * NZ), t), device_id_type=MESH)
        return carry

    lax.fori_loop(1, NX * NZ, greet, 0)
    for peer in (rep_at(y, 1 - xh, core), rep_at(y, xh, 1 - core), rep_at(y + 1, xh, core), rep_at(y + 3, xh, core)):
        pl.semaphore_signal(barrier, inc=1, device_id=peer, device_id_type=MESH)
    pl.semaphore_wait(barrier, NX * NZ - 1 + 4)

    def over_blk(n):
        e, rel = n // 2, n % 2 + n // 14
        x, zz = (xl + rel) % NX, (z + 2 * NZ - step_of(e)) % NZ
        to = x * NZ + zz
        return (
            pltpu.make_async_remote_copy(
                a_ref.at[:, to], g.at[me, e, rel], ga_send.at[e, rel], ga_recv.at[e, rel], device_id=(to, t), device_id_type=MESH
            ),
            pltpu.make_async_remote_copy(
                cols_ref.at[to], cols_v.at[e, rel], gc_send.at[e, rel], gc_recv.at[e, rel], device_id=(to, t), device_id_type=MESH
            ),
        )

    def send_blk(e):
        for copy in over_blk(2 * e + 1 - e // 7):
            copy.start()

        @pl.when(e < 7)
        def _():
            for copy in over_blk(2 * e):
                copy.start()

    for e in range(AHEAD):
        send_blk(jnp.int32(e))

    b[ZERO] = jnp.zeros((BS, BS), b.dtype)
    rd[DUMMY] = jnp.zeros(rd.shape[1:], rd.dtype)
    rs[DUMMY] = jnp.zeros(rs.shape[1:], rs.dtype)

    def one_piece(e, piece, n, to):
        return pltpu.make_async_remote_copy(
            g.at[piece, e], g.at[piece, e], rep_send.at[e, n], rep_recv.at[e, piece], device_id=to, device_id_type=MESH
        )

    def two_pieces(e, yy, c, n, to):
        first = slot(yy, 0, c)
        both = g.at[pl.ds(first, 2), e]
        return pltpu.make_async_remote_copy(
            both, both, rep_send.at[e, n], rep_recv.at[e, first], device_id=to, device_id_type=MESH
        )

    other_core = rep_at(y, xh, 1 - core)
    above, below = rep_at(y + 1, xh, core), rep_at(y + 3, xh, core)

    def first_sends(e):
        yield one_piece(e, me, 0, rep_at(y, 1 - xh, core))

    def second_sends(e):
        one_piece(e, slot(y, 1 - xh, core), 0, other_core).wait_recv()
        yield two_pieces(e, y, core, 1, above)
        yield two_pieces(e, y, core, 2, below)
        yield two_pieces(e, y, core, 3, other_core)

    def third_sends(e):
        two_pieces(e, y + 3, core, 0, other_core).wait_recv()
        yield one_piece(e, slot(y + 3, 0, core), 4, above)
        yield two_pieces(e, y + 3, core, 5, other_core)
        two_pieces(e, y + 1, core, 0, other_core).wait_recv()
        yield one_piece(e, slot(y + 1, 1, core), 6, below)
        yield two_pieces(e, y + 1, core, 7, other_core)

    def fourth_sends(e):
        for h in (0, 1):
            one_piece(e, slot(y + 2, h, core), 0, other_core).wait_recv()
        yield two_pieces(e, y + 2, core, 8, other_core)

    def stage_a(e):
        for rel in (1, 0):
            def remote():
                copies = over_blk(2 * e + rel - e // 7)
                for copy in copies:
                    copy.wait_recv()

            if rel:
                remote()
            else:
                pl.when(e < 7)(remote)

                @pl.when(e == 7)
                def _():
                    own_a.wait()
                    own_c.wait()

        pltpu.make_async_copy(cols_v.at[e], cols_s.at[e], cols_sem.at[e]).start()
        for copy in first_sends(e):
            copy.start()

    def stage_b(e):
        for copy in second_sends(e):
            copy.start()

    def stage_c(e):
        for copy in third_sends(e):
            copy.start()

    def stage_d(e):
        for copy in fourth_sends(e):
            copy.start()

    def multiply(e):
        for yy in range(NY):
            two_pieces(e, yy, 1 - core, 0, other_core).wait_recv()
        pltpu.make_async_copy(cols_v.at[e], cols_s.at[e], cols_sem.at[e]).wait()

        def one_rel(rel, carry):
            owner = ((xl + rel) % NX) * NZ + (z + step_of(e)) % NZ
            for r in range(ROWS):
                row = (owner * ROWS + r) * KC
                for s in range(KA):
                    k = cols_s[e, rel, r, s]
                    for c in range(KC):
                        which = table_s[row + c, k]
                        picked[r, pl.ds(s * BS, BS), pl.ds(c * BS, BS)] = b[which]
            for r in range(ROWS):
                left = g[:, e, rel, r].astype(jnp.float32).reshape(NC, NY * NXH, KA, BS // NREP, BS)
                left = [left[c, m, s] for s in range(KA) for m in range(NY * NXH) for c in range(NC)]
                left = jnp.concatenate(left, axis=0).astype(b.dtype)
                total = lax.dot_general(left, picked[r], (((0,), (0,)), ((), ())), preferred_element_type=jnp.float32)
                for c in range(KC):
                    part[rel, r, c] = total[:, c * BS : (c + 1) * BS]
            return carry

        lax.fori_loop(0, 2, one_rel, 0)

    def message(frm, to_slot, to):
        return (
            pltpu.make_async_remote_copy(sd.at[frm], rd.at[to_slot], d_send.at[frm], d_recv.at[to_slot], device_id=to, device_id_type=MESH),
            pltpu.make_async_remote_copy(ss.at[frm], rs.at[to_slot], s_send.at[frm], s_recv.at[to_slot], device_id=to, device_id_type=MESH),
        )

    def received(at):
        for copy in message(0, at, blk_at(1 - xl, z)):
            copy.wait_recv()

    def totals(rel, first_col, at, j):
        r, c = j // 2, first_col + j % 2
        low, high = part[rel, r, c, pl.ds(0, HALF)], part[rel, r, c, pl.ds(HALF, HALF)]
        for n in at:
            word, scale = rd[n, j], rs[n, pl.ds(j, 1)]
            low += ((word & 0xFFFF).astype(jnp.float32) - 32768.0) * scale
            high += (lax.shift_right_logical(word, 16).astype(jnp.float32) - 32768.0) * scale
        return low, high

    def pack(rel, first_col, at, to_slot):
        def one(j, carry):
            low, high = totals(rel, first_col, at, j)
            top = jnp.maximum(jnp.max(jnp.maximum(jnp.abs(low), jnp.abs(high)), axis=0, keepdims=True), 1e-33)
            gain = 32767.0 / top
            low = (low * gain + 32768.5).astype(jnp.int32)
            high = (high * gain + 32768.5).astype(jnp.int32)
            sd[to_slot, j] = low | (high << 16)
            ss[to_slot, pl.ds(j, 1)] = top * (1.0 / 32767.0)
            return carry

        lax.fori_loop(0, BLOCKS, one, 0)

    def keep(first_col, at):
        def one(j, carry):
            low, high = totals(0, first_col, at, j)
            r, c = j // 2, first_col + j % 2
            out_ref[r, c, pl.ds(0, HALF)] = low
            out_ref[r, c, pl.ds(HALF, HALF)] = high
            return carry

        lax.fori_loop(0, BLOCKS, one, 0)

    def z_slot(e, kind):
        return (e - 1) * 3 + kind

    def along_z(e, kind):
        up = jnp.where(e == 0, jnp.int32(kind != NEAR), e % 2)
        at = jnp.where(e == 0, 2 - up, e + 2)
        return message(e * 3 + kind, z_slot(at, kind), blk_at(xl, z + NZ + 2 * up - 1))

    def has_z(e, kind):
        return (e >= 3) | (e == (2 if kind == NEAR else 1))

    def pass_on(e, kind):
        at = [jnp.where(has_z(e, kind), z_slot(e, kind), DUMMY)]
        if kind == DONE:
            received(Z_RECVS + e)
            at.append(Z_RECVS + e)

        @pl.when(has_z(e, kind))
        def _():
            received(z_slot(e, kind))

        pack(int(kind == FAR), FIRST_COL[kind], at, e * 3 + kind)
        for copy in along_z(e, kind):
            copy.start()

    def across_x(n):
        return message(Z_SENDS + n, Z_RECVS + n, blk_at(1 - xl, z))

    def send_x(n, at, first_col):
        pack(1, first_col, at, Z_SENDS + n)
        for copy in across_x(n):
            copy.start()

    def one_step(i, carry):
        pl.when(i < 8)(lambda: stage_a(i))
        pl.when(i + AHEAD < 8)(lambda: send_blk(i + AHEAD))
        for lead, stage in ((LEAD_B, stage_b), (LEAD_C, stage_c), (LEAD_D, stage_d)):
            n = i - LEAD_A + lead
            pl.when((n >= 0) & (n < 8))(lambda stage=stage, n=n: stage(n))

        @pl.when(i >= LEAD_A)
        def _():
            e = i - LEAD_A
            pl.when(e >= 1)(lambda: pass_on(e - 1, DONE))

            @pl.when(e == 0)
            def _():
                load_b.wait()
                load_t.wait()

            multiply(e)
            send_x(e, [], FIRST_COL[DONE])

            @pl.when(e < 7)
            def _():
                pass_on(e, FAR)
                pass_on(e, NEAR)

        return carry

    lax.fori_loop(0, 8 + LEAD_A, one_step, 0)

    def last_z(kind):
        for e in (7, 8):
            received(z_slot(e, kind))
        return [z_slot(7, kind), z_slot(8, kind)]

    send_x(8, last_z(FAR), FIRST_COL[FAR])

    def sent_blk(n, carry):
        for copy in over_blk(n):
            copy.wait_send()
        return carry

    def sent_rep(e, carry):
        for n in (0, 4, 6):
            one_piece(e, me, n, other_core).wait_send()
        for n in (1, 2, 3, 5, 7, 8):
            two_pieces(e, y, core, n, other_core).wait_send()
        return carry

    def sent_messages(n, carry):
        for copy in message(n, 0, blk_at(1 - xl, z)):
            copy.wait_send()
        return carry

    lax.fori_loop(0, 15, sent_blk, 0)
    lax.fori_loop(0, 8, sent_rep, 0)
    received(Z_RECVS + 7)
    keep(FIRST_COL[DONE], last_z(DONE) + [Z_RECVS + 7])
    lax.fori_loop(0, Z_SENDS + X_SENDS - 1, sent_messages, 0)
    near = last_z(NEAR)
    received(Z_RECVS + 8)
    keep(FIRST_COL[NEAR], near + [Z_RECVS + 8])
    sent_messages(Z_SENDS + X_SENDS - 1, 0)


def per_device(a_blocks, a_cols, b_blocks, b_cols, c_cols):
    panels = a_blocks.shape[1]
    pieces = jnp.swapaxes(a_blocks, 3, 4).reshape(ROWS, panels, PIECE, BS)
    lists = jnp.pad(jnp.swapaxes(a_cols, 0, 1), ((0, 0), (0, 8 - ROWS), (0, 128 - KA)))
    wanted = c_cols[:, 0].reshape(-1, 1)
    have = jnp.pad(jnp.swapaxes(b_cols[:, 0], 0, 1), ((0, 0), (0, 128 - KP)), constant_values=-1)
    first = lax.broadcasted_iota(jnp.int32, (1, 128), 1) * KB
    table = jnp.full((wanted.shape[0], 128), ZERO, jnp.int32)
    for slot_t in range(KB):
        table = jnp.where(have[slot_t : slot_t + 1] == wanted, first + slot_t, table)
    any_ref = pl.BlockSpec(memory_space=pl.ANY)
    vmem = pltpu.VMEM
    dma = pltpu.SemaphoreType.DMA
    mine = pl.pallas_call(
        kernel,
        out_shape=jax.ShapeDtypeStruct((ROWS, KC, BS, BS), jnp.float32),
        in_specs=[any_ref] * 4,
        out_specs=pl.BlockSpec(memory_space=pltpu.VMEM),
        scratch_shapes=[
            vmem((NREP, 8, 2, ROWS, PIECE, BS), jnp.bfloat16),
            vmem((ZERO + 1, BS, BS), jnp.bfloat16),
            vmem((ROWS, KA * BS, KC * BS), jnp.bfloat16),
            vmem((2, ROWS, KC, BS, BS), jnp.float32),
            vmem((8, 2, 8, 128), jnp.int32),
            pltpu.SMEM((8, 2, 8, 128), jnp.int32),
            pltpu.SMEM((table.shape[0], 128), jnp.int32),
            vmem((Z_SENDS + X_SENDS, BLOCKS, HALF, BS), jnp.int32),
            vmem((Z_SENDS + X_SENDS, 8, BS), jnp.float32),
            vmem((DUMMY + 1, BLOCKS, HALF, BS), jnp.int32),
            vmem((DUMMY + 1, 8, BS), jnp.float32),
            dma((8, 2)), dma((8, 2)), dma((8, 2)), dma((8, 2)), dma((8,)), dma((4,)),
            dma((8, 9)), dma((8, NREP)),
            dma((Z_SENDS + X_SENDS,)), dma((Z_SENDS + X_SENDS,)), dma((DUMMY,)), dma((DUMMY,)),
        ],
        compiler_params=pltpu.CompilerParams(collective_id=0, has_side_effects=True, vmem_limit_bytes=56 * 2**20),
        name="block_product",
    )(pieces, lists, b_blocks.reshape(KP * KB, BS, BS), table)
    return mine.reshape(ROWS, 1, KC, BS, BS)


def solution(mesh):
    placed = (
        P("blk", None, None, None, "rep"),
        P("blk", None, None),
        P("blk", "rep", None, None, None),
        P("blk", "rep", None),
        P(None, "rep", None),
    )
    return jax.shard_map(
        per_device,
        mesh=mesh,
        in_specs=placed,
        out_specs=P("blk", "rep", None, None, None),
        check_vma=False,
    )
```

```python
import jax
import jax.numpy as jnp
from jax import lax
from jax.experimental import pallas as pl
from jax.experimental.pallas import tpu as pltpu
from jax.sharding import PartitionSpec as P

MESH = pl.DeviceIdType.MESH
NX, NZ = 2, 8
NY, NXH, NC = 4, 2, 2
NREP = NY * NXH * NC
ROWS, KA, KB, KC, BS, KP = 3, 6, 3, 4, 128, 112
HALF = BS // 2
PIECE = KA * BS // NREP
BLOCKS = ROWS * 2
ZERO = KP * KB
Z_SENDS, X_SENDS = 21, 9
Z_RECVS, X_RECVS = 24, 9
DUMMY = Z_RECVS + X_RECVS
FAR, NEAR, DONE = 0, 1, 2
FIRST_COL = (0, 0, 2)
LEAD_A, LEAD_B, LEAD_C, LEAD_D = 3, 2, 1, 0
AHEAD = 4


def step_of(e):
    far = (8 - e) // 2
    return far * (2 * (e % 2) - 1) + NZ


def kernel(
    a_ref, cols_ref, b_hbm, table_hbm, out_ref,
    g, b, picked, part, cols_v, cols_s, table_s, sd, ss, rd, rs,
    ga_send, ga_recv, gc_send, gc_recv, cols_sem, load_sem,
    rep_send, rep_recv, d_send, s_send, d_recv, s_recv,
):
    q, t = lax.axis_index("blk"), lax.axis_index("rep")
    xl, z = q // NZ, q % NZ
    y, xh, core = t // (NXH * NC), (t // NC) % NXH, t % NC

    def blk_at(x, zz):
        return (x * NZ + zz % NZ, t)

    def rep_at(yy, h, c):
        return (q, (yy % NY) * (NXH * NC) + h * NC + c)

    def slot(yy, h, c):
        return c * (NY * NXH) + (yy % NY) * NXH + h

    me = slot(y, xh, core)

    load_b = pltpu.make_async_copy(b_hbm, b.at[pl.ds(0, ZERO)], load_sem.at[0])
    load_t = pltpu.make_async_copy(table_hbm, table_s, load_sem.at[1])
    load_b.start()
    load_t.start()
    own_a = pltpu.make_async_copy(a_ref.at[:, q], g.at[me, 7, 0], load_sem.at[2])
    own_c = pltpu.make_async_copy(cols_ref.at[q], cols_v.at[7, 0], load_sem.at[3])
    own_a.start()
    own_c.start()

    barrier = pltpu.get_barrier_semaphore()

    def greet(n, carry):
        pl.semaphore_signal(barrier, inc=1, device_id=((q + n) % (NX * NZ), t), device_id_type=MESH)
        return carry

    lax.fori_loop(1, NX * NZ, greet, 0)
    for peer in (rep_at(y, 1 - xh, core), rep_at(y, xh, 1 - core), rep_at(y + 1, xh, core), rep_at(y + 3, xh, core)):
        pl.semaphore_signal(barrier, inc=1, device_id=peer, device_id_type=MESH)
    pl.semaphore_wait(barrier, NX * NZ - 1 + 4)

    def over_blk(n):
        e, rel = n // 2, n % 2 + n // 14
        x, zz = (xl + rel) % NX, (z + 2 * NZ - step_of(e)) % NZ
        to = x * NZ + zz
        return (
            pltpu.make_async_remote_copy(
                a_ref.at[:, to], g.at[me, e, rel], ga_send.at[e, rel], ga_recv.at[e, rel], device_id=(to, t), device_id_type=MESH
            ),
            pltpu.make_async_remote_copy(
                cols_ref.at[to], cols_v.at[e, rel], gc_send.at[e, rel], gc_recv.at[e, rel], device_id=(to, t), device_id_type=MESH
            ),
        )

    def send_blk(e):
        for copy in over_blk(2 * e + 1 - e // 7):
            copy.start()

        @pl.when(e < 7)
        def _():
            for copy in over_blk(2 * e):
                copy.start()

    for e in range(AHEAD):
        send_blk(jnp.int32(e))

    b[ZERO] = jnp.zeros((BS, BS), b.dtype)
    rd[DUMMY] = jnp.zeros(rd.shape[1:], rd.dtype)
    rs[DUMMY] = jnp.zeros(rs.shape[1:], rs.dtype)

    def one_piece(e, piece, n, to):
        return pltpu.make_async_remote_copy(
            g.at[piece, e], g.at[piece, e], rep_send.at[e, n], rep_recv.at[e, piece], device_id=to, device_id_type=MESH
        )

    def two_pieces(e, yy, c, n, to):
        first = slot(yy, 0, c)
        both = g.at[pl.ds(first, 2), e]
        return pltpu.make_async_remote_copy(
            both, both, rep_send.at[e, n], rep_recv.at[e, first], device_id=to, device_id_type=MESH
        )

    other_core = rep_at(y, xh, 1 - core)
    above, below = rep_at(y + 1, xh, core), rep_at(y + 3, xh, core)

    def first_sends(e):
        yield one_piece(e, me, 0, rep_at(y, 1 - xh, core))

    def second_sends(e):
        one_piece(e, slot(y, 1 - xh, core), 0, other_core).wait_recv()
        yield two_pieces(e, y, core, 1, above)
        yield two_pieces(e, y, core, 2, below)
        yield two_pieces(e, y, core, 3, other_core)

    def third_sends(e):
        two_pieces(e, y + 3, core, 0, other_core).wait_recv()
        yield one_piece(e, slot(y + 3, 0, core), 4, above)
        yield two_pieces(e, y + 3, core, 5, other_core)
        two_pieces(e, y + 1, core, 0, other_core).wait_recv()
        yield one_piece(e, slot(y + 1, 1, core), 6, below)
        yield two_pieces(e, y + 1, core, 7, other_core)

    def fourth_sends(e):
        for h in (0, 1):
            one_piece(e, slot(y + 2, h, core), 0, other_core).wait_recv()
        yield two_pieces(e, y + 2, core, 8, other_core)

    def stage_a(e):
        for rel in (1, 0):
            def remote():
                copies = over_blk(2 * e + rel - e // 7)
                for copy in copies:
                    copy.wait_recv()

            if rel:
                remote()
            else:
                pl.when(e < 7)(remote)

                @pl.when(e == 7)
                def _():
                    own_a.wait()
                    own_c.wait()

        pltpu.make_async_copy(cols_v.at[e], cols_s.at[e], cols_sem.at[e]).start()
        for copy in first_sends(e):
            copy.start()

    def stage_b(e):
        for copy in second_sends(e):
            copy.start()

    def stage_c(e):
        for copy in third_sends(e):
            copy.start()

    def stage_d(e):
        for copy in fourth_sends(e):
            copy.start()

    def multiply(e):
        for yy in range(NY):
            two_pieces(e, yy, 1 - core, 0, other_core).wait_recv()
        pltpu.make_async_copy(cols_v.at[e], cols_s.at[e], cols_sem.at[e]).wait()

        def one_rel(rel, carry):
            owner = ((xl + rel) % NX) * NZ + (z + step_of(e)) % NZ
            for r in range(ROWS):
                row = (owner * ROWS + r) * KC
                for s in range(KA):
                    k = cols_s[e, rel, r, s]
                    for c in range(KC):
                        which = table_s[row + c, k]
                        picked[r, pl.ds(s * BS, BS), pl.ds(c * BS, BS)] = b[which]
            for r in range(ROWS):
                left = g[:, e, rel, r].astype(jnp.float32).reshape(NC, NY * NXH, KA, BS // NREP, BS)
                left = [left[c, m, s] for s in range(KA) for m in range(NY * NXH) for c in range(NC)]
                left = jnp.concatenate(left, axis=0).astype(b.dtype)
                total = lax.dot_general(left, picked[r], (((0,), (0,)), ((), ())), preferred_element_type=jnp.float32)
                for c in range(KC):
                    part[rel, r, c] = total[:, c * BS : (c + 1) * BS]
            return carry

        lax.fori_loop(0, 2, one_rel, 0)

    def message(frm, to_slot, to):
        return (
            pltpu.make_async_remote_copy(sd.at[frm], rd.at[to_slot], d_send.at[frm], d_recv.at[to_slot], device_id=to, device_id_type=MESH),
            pltpu.make_async_remote_copy(ss.at[frm], rs.at[to_slot], s_send.at[frm], s_recv.at[to_slot], device_id=to, device_id_type=MESH),
        )

    def received(at):
        for copy in message(0, at, blk_at(1 - xl, z)):
            copy.wait_recv()

    def totals(rel, first_col, at, j):
        r, c = j // 2, first_col + j % 2
        low, high = part[rel, r, c, pl.ds(0, HALF)], part[rel, r, c, pl.ds(HALF, HALF)]
        for n in at:
            word, scale = rd[n, j], rs[n, pl.ds(j, 1)]
            low += ((word & 0xFFFF).astype(jnp.float32) - 32768.0) * scale
            high += (lax.shift_right_logical(word, 16).astype(jnp.float32) - 32768.0) * scale
        return low, high

    def pack(rel, first_col, at, to_slot):
        def one(j, carry):
            low, high = totals(rel, first_col, at, j)
            top = jnp.maximum(jnp.max(jnp.maximum(jnp.abs(low), jnp.abs(high)), axis=0, keepdims=True), 1e-33)
            gain = 32767.0 / top
            low = (low * gain + 32768.5).astype(jnp.int32)
            high = (high * gain + 32768.5).astype(jnp.int32)
            sd[to_slot, j] = low | (high << 16)
            ss[to_slot, pl.ds(j, 1)] = top * (1.0 / 32767.0)
            return carry

        lax.fori_loop(0, BLOCKS, one, 0)

    def keep(first_col, at):
        def one(j, carry):
            low, high = totals(0, first_col, at, j)
            r, c = j // 2, first_col + j % 2
            out_ref[r, c, pl.ds(0, HALF)] = low
            out_ref[r, c, pl.ds(HALF, HALF)] = high
            return carry

        lax.fori_loop(0, BLOCKS, one, 0)

    def z_slot(e, kind):
        return (e - 1) * 3 + kind

    def along_z(e, kind):
        up = jnp.where(e == 0, jnp.int32(kind != NEAR), e % 2)
        at = jnp.where(e == 0, 2 - up, e + 2)
        return message(e * 3 + kind, z_slot(at, kind), blk_at(xl, z + NZ + 2 * up - 1))

    def has_z(e, kind):
        return (e >= 3) | (e == (2 if kind == NEAR else 1))

    def pass_on(e, kind):
        at = [jnp.where(has_z(e, kind), z_slot(e, kind), DUMMY)]
        if kind == DONE:
            received(Z_RECVS + e)
            at.append(Z_RECVS + e)

        @pl.when(has_z(e, kind))
        def _():
            received(z_slot(e, kind))

        pack(int(kind == FAR), FIRST_COL[kind], at, e * 3 + kind)
        for copy in along_z(e, kind):
            copy.start()

    def across_x(n):
        return message(Z_SENDS + n, Z_RECVS + n, blk_at(1 - xl, z))

    def send_x(n, at, first_col):
        pack(1, first_col, at, Z_SENDS + n)
        for copy in across_x(n):
            copy.start()

    def one_step(i, carry):
        for lead, stage in ((LEAD_D, stage_d), (LEAD_C, stage_c), (LEAD_B, stage_b)):
            n = i - LEAD_A + lead
            pl.when((n >= 0) & (n < 8))(lambda stage=stage, n=n: stage(n))
        pl.when(i < 8)(lambda: stage_a(i))
        pl.when(i + AHEAD < 8)(lambda: send_blk(i + AHEAD))

        @pl.when(i >= LEAD_A)
        def _():
            e = i - LEAD_A
            pl.when(e >= 1)(lambda: pass_on(e - 1, DONE))

            @pl.when(e == 0)
            def _():
                load_b.wait()
                load_t.wait()

            multiply(e)
            send_x(e, [], FIRST_COL[DONE])

            @pl.when(e < 7)
            def _():
                pass_on(e, FAR)
                pass_on(e, NEAR)

        return carry

    lax.fori_loop(0, 8 + LEAD_A, one_step, 0)

    def last_z(kind):
        for e in (7, 8):
            received(z_slot(e, kind))
        return [z_slot(7, kind), z_slot(8, kind)]

    send_x(8, last_z(FAR), FIRST_COL[FAR])

    def sent_blk(n, carry):
        for copy in over_blk(n):
            copy.wait_send()
        return carry

    def sent_rep(e, carry):
        for n in (0, 4, 6):
            one_piece(e, me, n, other_core).wait_send()
        for n in (1, 2, 3, 5, 7, 8):
            two_pieces(e, y, core, n, other_core).wait_send()
        return carry

    def sent_messages(n, carry):
        for copy in message(n, 0, blk_at(1 - xl, z)):
            copy.wait_send()
        return carry

    lax.fori_loop(0, 15, sent_blk, 0)
    lax.fori_loop(0, 8, sent_rep, 0)
    received(Z_RECVS + 7)
    keep(FIRST_COL[DONE], last_z(DONE) + [Z_RECVS + 7])
    lax.fori_loop(0, Z_SENDS + X_SENDS - 1, sent_messages, 0)
    near = last_z(NEAR)
    received(Z_RECVS + 8)
    keep(FIRST_COL[NEAR], near + [Z_RECVS + 8])
    sent_messages(Z_SENDS + X_SENDS - 1, 0)


def per_device(a_blocks, a_cols, b_blocks, b_cols, c_cols):
    panels = a_blocks.shape[1]
    pieces = jnp.swapaxes(a_blocks, 3, 4).reshape(ROWS, panels, PIECE, BS)
    lists = jnp.pad(jnp.swapaxes(a_cols, 0, 1), ((0, 0), (0, 8 - ROWS), (0, 128 - KA)))
    wanted = c_cols[:, 0].reshape(-1, 1)
    have = jnp.pad(jnp.swapaxes(b_cols[:, 0], 0, 1), ((0, 0), (0, 128 - KP)), constant_values=-1)
    first = lax.broadcasted_iota(jnp.int32, (1, 128), 1) * KB
    table = jnp.full((wanted.shape[0], 128), ZERO, jnp.int32)
    for slot_t in range(KB):
        table = jnp.where(have[slot_t : slot_t + 1] == wanted, first + slot_t, table)
    any_ref = pl.BlockSpec(memory_space=pl.ANY)
    vmem = pltpu.VMEM
    dma = pltpu.SemaphoreType.DMA
    mine = pl.pallas_call(
        kernel,
        out_shape=jax.ShapeDtypeStruct((ROWS, KC, BS, BS), jnp.float32),
        in_specs=[any_ref] * 4,
        out_specs=pl.BlockSpec(memory_space=pltpu.VMEM),
        scratch_shapes=[
            vmem((NREP, 8, 2, ROWS, PIECE, BS), jnp.bfloat16),
            vmem((ZERO + 1, BS, BS), jnp.bfloat16),
            vmem((ROWS, KA * BS, KC * BS), jnp.bfloat16),
            vmem((2, ROWS, KC, BS, BS), jnp.float32),
            vmem((8, 2, 8, 128), jnp.int32),
            pltpu.SMEM((8, 2, 8, 128), jnp.int32),
            pltpu.SMEM((table.shape[0], 128), jnp.int32),
            vmem((Z_SENDS + X_SENDS, BLOCKS, HALF, BS), jnp.int32),
            vmem((Z_SENDS + X_SENDS, 8, BS), jnp.float32),
            vmem((DUMMY + 1, BLOCKS, HALF, BS), jnp.int32),
            vmem((DUMMY + 1, 8, BS), jnp.float32),
            dma((8, 2)), dma((8, 2)), dma((8, 2)), dma((8, 2)), dma((8,)), dma((4,)),
            dma((8, 9)), dma((8, NREP)),
            dma((Z_SENDS + X_SENDS,)), dma((Z_SENDS + X_SENDS,)), dma((DUMMY,)), dma((DUMMY,)),
        ],
        compiler_params=pltpu.CompilerParams(collective_id=0, has_side_effects=True, vmem_limit_bytes=56 * 2**20),
        name="block_product",
    )(pieces, lists, b_blocks.reshape(KP * KB, BS, BS), table)
    return mine.reshape(ROWS, 1, KC, BS, BS)


def solution(mesh):
    placed = (
        P("blk", None, None, None, "rep"),
        P("blk", None, None),
        P("blk", "rep", None, None, None),
        P("blk", "rep", None),
        P(None, "rep", None),
    )
    return jax.shard_map(
        per_device,
        mesh=mesh,
        in_specs=placed,
        out_specs=P("blk", "rep", None, None, None),
        check_vma=False,
    )
```
